256 devices in a mesh: group: 8 (over z_hi, y), blk: 32 (over x, z_lo, core).
Axes of the slice: x: 4, y: 4, z: 8 (z_hi: 2, z_lo: 4; z = z_hi * 4 + z_lo), core: 2. Of those that a mesh axis runs over, the one named last changes fastest.
Arguments:
- picture_embeddings: float32 [16384, 1152], P('blk'), may hold values from -4 to 4
- caption_embeddings: float32 [16384, 1152], P(('group', 'blk')), may hold values from -4 to 4
- exponent_of_sharpness: float32 [1], replicated, may hold values from 2.2 to 2.8
- offset_shift: float32 [1], replicated, may hold values from -9 to -6
Outputs:
- picture_embedding_slope: float32 [16384, 1152], P('blk')
- text_grad: float32 [16384, 1152], P(('group', 'blk'))
- statistics: float32 [3], replicated
The draws below stay inside these ranges and needn't reach their ends.
All inputs are finite; a program needn't handle non-finite values.
Results may differ from the reference program's by a relative error of at most 0.0015.
Values may be sent and summed in bfloat16 or wider, within the bound.
No kernel may reach another device: no remote copies, remote signals or barrier semaphores. Data moves between devices by JAX's collectives and lax.ppermute only.
A program may use at most 64 MiB of HBM per device.

```python
import math
import jax
import jax.numpy as jnp
from jax import lax

D = 1152
PAIR_BATCH = 16384


def shared_parts(key, feature_top, intensity_beginning, strength_end):
    feature_key = jax.random.fold_in(key, 101)
    topic_key = jax.random.fold_in(key, 102)
    label_key = jax.random.fold_in(key, 103)
    spread_key = jax.random.fold_in(key, 104)
    noise_key = jax.random.fold_in(key, 105)
    feature_scale = jnp.exp(jax.random.uniform(feature_key, (D,), jnp.float32, 0.0, math.log(feature_top)))
    topics = jax.random.truncated_normal(topic_key, -3.0, 3.0, (64, D), jnp.float32)
    labels = jax.random.randint(label_key, (PAIR_BATCH,), 0, 64)
    position = jnp.arange(PAIR_BATCH, dtype=jnp.float32) / PAIR_BATCH
    strength = (intensity_beginning + (strength_end - intensity_beginning) * position) * jax.random.uniform(spread_key, (PAIR_BATCH,), jnp.float32, 0.8, 1.2)
    shared_noise = jax.random.truncated_normal(noise_key, -3.0, 3.0, (PAIR_BATCH, D), jnp.float32)
    signal = strength[:, None] * topics[labels]
    return (feature_scale, signal, shared_noise)


def draw_picture_embeddings(key, part):
    feature_scale, signal, shared_noise = shared_parts(key, 10.0, 0.3, 1.2)
    row_top = 10.0
    key = jax.random.fold_in(key, 1)
    row_scale = jnp.exp(jax.random.uniform(key, (PAIR_BATCH, 1), jnp.float32, 0.0, math.log(row_top)))
    return 0.0015 * row_scale * feature_scale[None, :] * (signal + shared_noise)


def draw_caption_embeddings(key, part):
    feature_scale, signal, shared_noise = shared_parts(key, 10.0, 0.3, 1.2)
    row_top = 10.0
    key = jax.random.fold_in(key, 2)
    scale_key = jax.random.fold_in(key, 11)
    own_key = jax.random.fold_in(key, 12)
    row_scale = jnp.exp(jax.random.uniform(scale_key, (PAIR_BATCH, 1), jnp.float32, 0.0, math.log(row_top)))
    own_noise = jax.random.truncated_normal(own_key, -3.0, 3.0, (PAIR_BATCH, D), jnp.float32)
    return 0.0015 * row_scale * feature_scale[None, :] * (signal + 0.6 * shared_noise + 0.8 * own_noise)


def setup_inputs(seed: int = 0) -> dict:
    streams_of = jax.random.split(jax.random.key(seed), 5)
    return {
        "picture_embeddings": draw_picture_embeddings(jax.random.fold_in(streams_of[4], 71), 0),
        "caption_embeddings": draw_caption_embeddings(jax.random.fold_in(streams_of[4], 71), 0),
        "exponent_of_sharpness": jnp.clip(jax.random.uniform(streams_of[2], (1,), jnp.float32, 2.2, 2.8), 2.2, 2.8),
        "offset_shift": jnp.clip(jax.random.uniform(streams_of[3], (1,), jnp.float32, -9.0, -6.0), -9.0, -6.0),
    }


def normalize_rows(matrix):
    inverse_norm = lax.rsqrt(lax.optimization_barrier(jnp.sum(matrix * matrix, axis=1, keepdims=True)) + 1e-06)
    return (matrix * inverse_norm, inverse_norm)

def unit_backward(grad, unit_rows, inverse_norm):
    return (grad - unit_rows * lax.optimization_barrier(jnp.sum(unit_rows * grad, axis=1, keepdims=True))) * inverse_norm

def reference(picture_embeddings, caption_embeddings, exponent_of_sharpness, offset_shift):
    unit_image, inv_image = normalize_rows(picture_embeddings)
    unit_text, inv_text = normalize_rows(caption_embeddings)
    image_rows = unit_image.astype(jnp.bfloat16)
    text_matrix_rows = unit_text.astype(jnp.bfloat16)
    sharpness_factor = jnp.exp(exponent_of_sharpness[0])
    block_rows = min(PAIR_BATCH, 1024)
    block_count = PAIR_BATCH // block_rows
    image_blocks = image_rows.reshape(block_count, block_rows, image_rows.shape[1])

    def visit(carry, inputs):
        text_total, partial_sums = carry
        block_slice, index = inputs
        dot_products = jnp.dot(block_slice, text_matrix_rows.T, preferred_element_type=jnp.float32)
        row_ids = lax.broadcasted_iota(jnp.int32, dot_products.shape, 0) + index * block_rows
        column_ids = lax.broadcasted_iota(jnp.int32, dot_products.shape, 1)
        signs = jnp.where(row_ids == column_ids, 1.0, -1.0).astype(jnp.float32)
        logit_matrix = sharpness_factor * dot_products + offset_shift[0]
        pair_loss = jax.nn.softplus(-signs * logit_matrix)
        coeff = -signs * jax.nn.sigmoid(-signs * logit_matrix)
        coefficient_rows = coeff.astype(jnp.bfloat16)
        image_portion = sharpness_factor * jnp.dot(coefficient_rows, text_matrix_rows, preferred_element_type=jnp.float32)
        text_portion = sharpness_factor * jnp.dot(coefficient_rows.T, block_slice, preferred_element_type=jnp.float32)
        new_sums = partial_sums + jnp.stack([jnp.sum(pair_loss), jnp.sum(coeff * dot_products), jnp.sum(coeff)])
        return ((text_total + text_portion, new_sums), image_portion)
    start = (jnp.zeros(caption_embeddings.shape, jnp.float32), jnp.zeros((3,), jnp.float32))
    indices = jnp.arange(block_count, dtype=jnp.int32)
    (text_unit_grad, partial_sums), image_parts = lax.scan(visit, start, (image_blocks, indices))
    image_unit_grad = image_parts.reshape(picture_embeddings.shape)
    statistics = jnp.stack([partial_sums[0], sharpness_factor * partial_sums[1], partial_sums[2]]) / PAIR_BATCH
    picture_embedding_slope = unit_backward(image_unit_grad, unit_image, inv_image)
    text_grad = unit_backward(text_unit_grad, unit_text, inv_text)
    return (picture_embedding_slope, text_grad, statistics)
```

```python
import jax
import jax.numpy as jnp
from jax import lax
from jax.experimental import pallas as pl
from jax.experimental.pallas import tpu as pltpu
from jax.sharding import PartitionSpec as P

AXES = ("group", "blk")
NEAR = (0, -1, 1, 2)
SEND = jnp.float16


def device_index(z, y, x, core):
    return (((z // 4) * 4 + y) * 4 + x) * 8 + (z % 4) * 2 + core


def shifted(dz=0, dy=0, dx=0, swap=0):
    pairs = []
    for z in range(8):
        for y in range(4):
            for x in range(4):
                for core in range(2):
                    there = device_index((z + dz) % 8, (y + dy) % 4, (x + dx) % 4, core ^ swap)
                    pairs.append((device_index(z, y, x, core), there))
    return pairs


def move(value, **shift):
    return lax.ppermute(value, AXES, shifted(**shift))


def normalize_rows(matrix):
    inverse_norm = lax.rsqrt(jnp.sum(matrix * matrix, axis=1, keepdims=True) + 1e-06)
    return (matrix * inverse_norm, inverse_norm)


def fused_kernel(row_chunk, scal_ref, base_ref, ids_ref, other_ref, own_ref, text_ref,
                 gi_ref, gt_ref, stat_ref, coef_ref, image_ref):
    step = pl.program_id(0)
    half = pl.num_programs(0) // 2
    bias = scal_ref[1]
    temperature = scal_ref[0]
    first = jnp.where(step < half, base_ref[0], base_ref[1]) + (step % half) * row_chunk
    rows = pl.ds(pl.multiple_of(step * row_chunk, row_chunk), row_chunk)

    @pl.when(step < half)
    def _():
        image_ref[rows, :] = other_ref[...]

    @pl.when(step >= half)
    def _():
        image_ref[rows, :] = own_ref[...]

    text = text_ref[...]
    products = lax.dot_general(
        image_ref[rows, :], text, (((1,), (1,)), ((), ())), preferred_element_type=jnp.float32
    )
    logits = temperature * products + bias
    row_ids = lax.broadcasted_iota(jnp.int32, products.shape, 0) + first
    paired = row_ids == ids_ref[...]
    negated = jnp.where(paired, -logits, logits)
    decay = jnp.exp(-jnp.abs(negated))
    loss = jnp.maximum(negated, 0.0) + jnp.log1p(decay)
    share = 1.0 / (1.0 + decay)
    sigmoid = jnp.where(negated >= 0.0, share, decay * share)
    coeff = jnp.where(paired, -sigmoid, sigmoid)
    coef_ref[rows, :] = coeff.astype(jnp.bfloat16)
    gi_ref[...] = jnp.dot(coef_ref[rows, :], text, preferred_element_type=jnp.float32)

    @pl.when(step == 0)
    def _():
        stat_ref[...] = jnp.zeros_like(stat_ref)

    width = products.shape[1]
    stat_ref[0] += jnp.sum(loss.reshape(-1, 8, width), axis=0)
    stat_ref[1] += jnp.sum((coeff * products).reshape(-1, 8, width), axis=0)
    stat_ref[2] += jnp.sum(coeff.reshape(-1, 8, width), axis=0)

    @pl.when(step == pl.num_programs(0) - 1)
    def _():
        gt_ref[...] = lax.dot_general(
            coef_ref[...], image_ref[...], (((0,), (0,)), ((), ())), preferred_element_type=jnp.float32
        )


def pair_terms(scalars, bases, ids, other, own, text, row_chunk=256):
    count, width = own.shape
    texts = text.shape[0]
    half = count // row_chunk
    return pl.pallas_call(
        lambda *refs: fused_kernel(row_chunk, *refs),
        grid=(2 * half,),
        in_specs=[
            pl.BlockSpec(memory_space=pltpu.SMEM),
            pl.BlockSpec(memory_space=pltpu.SMEM),
            pl.BlockSpec((1, texts), lambda i: (0, 0)),
            pl.BlockSpec((row_chunk, width), lambda i: (jnp.minimum(i, half - 1), 0)),
            pl.BlockSpec((row_chunk, width), lambda i: (jnp.maximum(i - half, 0), 0)),
            pl.BlockSpec((texts, width), lambda i: (0, 0)),
        ],
        out_specs=[
            pl.BlockSpec((row_chunk, width), lambda i: (i, 0)),
            pl.BlockSpec((texts, width), lambda i: (0, 0)),
            pl.BlockSpec((3, 8, texts), lambda i: (0, 0, 0)),
        ],
        out_shape=[
            jax.ShapeDtypeStruct((2 * count, width), jnp.float32),
            jax.ShapeDtypeStruct((texts, width), jnp.float32),
            jax.ShapeDtypeStruct((3, 8, texts), jnp.float32),
        ],
        scratch_shapes=[
            pltpu.VMEM((2 * count, texts), jnp.bfloat16),
            pltpu.VMEM((2 * count, width), jnp.bfloat16),
        ],
        compiler_params=pltpu.CompilerParams(vmem_limit_bytes=48 * 1024 * 1024),
        cost_estimate=pl.CostEstimate(
            flops=12 * count * texts * width, bytes_accessed=24 * count * width, transcendentals=6 * count * texts
        ),
    )(scalars, bases, ids, other, own, text)


def per_device(picture_embeddings, caption_embeddings, exponent_of_sharpness, offset_shift):
    count, width = picture_embeddings.shape
    group, blk = lax.axis_index("group"), lax.axis_index("blk")
    z, y, x, core = (group // 4) * 4 + (blk // 2) % 4, group % 4, blk // 8, blk % 2

    unit_text, inv_text = normalize_rows(caption_embeddings)
    text_rows = unit_text.astype(jnp.bfloat16)
    unit_image, inv_image = normalize_rows(picture_embeddings)
    image_rows = unit_image.astype(jnp.bfloat16)
    other_rows = move(image_rows, swap=1)

    n = caption_embeddings.shape[0]
    q = n // 4
    low, high = text_rows[: 2 * q], text_rows[2 * q :]
    low_x = [low, move(low, dx=1), move(low, dx=-1), move(low, dx=2)]
    high_z = [
        high,
        move(high, dz=1),
        move(high, dz=-1),
        move(high[:q], dz=2),
        move(high[q:], dz=-2),
    ]
    low_a = jnp.concatenate([v[:q] for v in low_x])
    low_b = jnp.concatenate([v[q:] for v in low_x])
    low_all = jnp.concatenate([low_a, low_b])
    low_z = [low_all, move(low_all, dz=1), move(low_all, dz=-1), move(low_a, dz=2), move(low_b, dz=-2)]
    high_all = jnp.concatenate(high_z)
    high_x = [high_all, move(high_all, dx=1), move(high_all, dx=-1), move(high_all, dx=2)]

    pieces, ids = [], []
    steps = jnp.arange(n, dtype=jnp.int32)
    for k, dx in enumerate(NEAR):
        at = (x + dx) % 4
        for j, dz in enumerate((0, -1, 1, -2, 2)):
            start = device_index((z + dz) % 8, y, at, core) * n
            own = start + steps
            a_low, b_low = slice(k * q, (k + 1) * q), slice(4 * q + k * q, 4 * q + (k + 1) * q)
            if j < 3:
                pieces += [low_z[j][a_low], low_z[j][b_low], high_x[k][2 * q * j : 2 * q * (j + 1)]]
                ids += [own]
            elif j == 3:
                pieces += [low_z[3][a_low], high_x[k][6 * q : 7 * q]]
                ids += [own[:q], own[2 * q : 3 * q]]
            else:
                pieces += [low_z[4][a_low], high_x[k][7 * q : 8 * q]]
                ids += [own[q : 2 * q], own[3 * q :]]
    texts = jnp.concatenate(pieces)
    text_ids = jnp.concatenate(ids)[None]

    temperature = jnp.exp(exponent_of_sharpness[0])
    scalars = jnp.stack([temperature, offset_shift[0]])
    bases = jnp.stack([(blk ^ 1) * count, blk * count]).astype(jnp.int32)
    image_terms, text_terms, sums = pair_terms(scalars, bases, text_ids, other_rows, image_rows, texts)

    quarter = count // 4
    received = move(image_terms[:count].astype(SEND), swap=1)
    chip_sum = (image_terms[count:] + received.astype(jnp.float32)).astype(SEND)
    part = lambda dy: lax.dynamic_slice_in_dim(chip_sum, ((y + dy) % 4) * quarter, quarter)
    y_sum = part(0).astype(jnp.float32)
    for dy in (1, -1, 2):
        y_sum += move(part(dy), dy=dy).astype(jnp.float32)
    y_sum = y_sum.astype(SEND)
    image_grad = y_sum.astype(jnp.float32) + move(y_sum, dz=4).astype(jnp.float32)
    unit_part = lax.dynamic_slice_in_dim(unit_image, y * quarter, quarter)
    tangent = (image_grad - unit_part * jnp.sum(unit_part * image_grad, axis=1, keepdims=True)).astype(SEND)
    slope = jnp.zeros((count, width), SEND)
    for dy in (0, 1, -1, 2):
        got = tangent if dy == 0 else move(tangent, dy=dy)
        slope = lax.dynamic_update_slice_in_dim(slope, got, ((y - dy) % 4) * quarter, 0)
    picture_embedding_slope = slope.astype(jnp.float32) * (temperature * inv_image)

    blocks = text_terms.reshape(4, 4 * n, width)
    x_sum = blocks[0]
    for k, dx in ((1, -1), (2, 1), (3, 2)):
        x_sum += move(blocks[k].astype(SEND), dx=dx).astype(jnp.float32)
    text_sum = x_sum[:n]
    z_send = x_sum[n:].astype(SEND)
    text_sum += move(z_send[:n], dz=-1).astype(jnp.float32)
    text_sum += move(z_send[n : 2 * n], dz=1).astype(jnp.float32)
    from_a = move(z_send[2 * n : 2 * n + 2 * q], dz=-2).astype(jnp.float32)
    from_b = move(z_send[2 * n + 2 * q :], dz=2).astype(jnp.float32)
    text_sum += jnp.concatenate([from_a[:q], from_b[:q], from_a[q:], from_b[q:]])
    text_grad = (
        (text_sum - unit_text * jnp.sum(unit_text * text_sum, axis=1, keepdims=True)) * (temperature * inv_text)
    )

    total = jnp.sum(sums.reshape(3, -1, 128), axis=1)
    total = jnp.concatenate([total, jnp.zeros((5, 128), jnp.float32)])
    for bit in range(8):
        pairs = [(i, i ^ (1 << bit)) for i in range(256)]
        total += lax.ppermute(total, AXES, pairs)
    total = jnp.sum(total, axis=1)
    rows_overall = count * lax.axis_size("blk")
    statistics = jnp.stack([total[0], temperature * total[1], total[2]]) / rows_overall
    return (picture_embedding_slope, text_grad, statistics)


def solution(mesh):
    placed = (P("blk", None), P(("group", "blk"), None), P(), P())
    return jax.shard_map(
        per_device,
        mesh=mesh,
        in_specs=placed,
        out_specs=(P("blk", None), P(("group", "blk"), None), P()),
        check_vma=False,
    )
```

```python
import jax
import jax.numpy as jnp
from jax import lax
from jax.experimental import pallas as pl
from jax.experimental.pallas import tpu as pltpu
from jax.sharding import PartitionSpec as P

AXES = ("group", "blk")
SEND = jnp.float16
VMEM_BYTES = 58 * 1024 * 1024
PAIR_VMEM_BYTES = 44 * 1024 * 1024
SMEM = pl.BlockSpec(memory_space=pltpu.SMEM)
HBM = pl.BlockSpec(memory_space=pltpu.HBM)


def device_index(z, y, x, core):
    return (((z // 4) * 4 + y) * 4 + x) * 8 + (z % 4) * 2 + core


def shifted(dz=0, dy=0, dx=0, swap=0):
    pairs = []
    for z in range(8):
        for y in range(4):
            for x in range(4):
                for core in range(2):
                    there = device_index((z + dz) % 8, (y + dy) % 4, (x + dx) % 4, core ^ swap)
                    pairs.append((device_index(z, y, x, core), there))
    return pairs


def move(value, **shift):
    return lax.ppermute(value, AXES, shifted(**shift))


def normalize_rows(matrix):
    inverse_norm = lax.rsqrt(jnp.sum(matrix * matrix, axis=1, keepdims=True) + 1e-06)
    return (matrix * inverse_norm, inverse_norm)


def text_kernel(text_ref, rows_ref, a_ref, b_ref):
    text = text_ref[...]
    rows = (text * lax.rsqrt(jnp.sum(text * text, axis=1, keepdims=True) + 1e-06)).astype(jnp.bfloat16)
    half = a_ref.shape[0]
    rows_ref[...] = rows
    a_ref[...] = rows[:half]
    b_ref[...] = rows[half:]


def text_messages(texts):
    n, width = texts.shape
    shape = lambda rows: jax.ShapeDtypeStruct((rows, width), jnp.bfloat16)
    return pl.pallas_call(
        text_kernel,
        grid=(1,),
        in_specs=[pl.BlockSpec((n, width), lambda i: (0, 0))],
        out_specs=[pl.BlockSpec((rows, width), lambda i: (0, 0)) for rows in (n, n // 2, n // 2)],
        out_shape=[shape(n), shape(n // 2), shape(n // 2)],
        compiler_params=pltpu.CompilerParams(vmem_limit_bytes=VMEM_BYTES),
        name="text_rows",
    )(texts)


def run_copies(pairs, sems):
    copies = [pltpu.make_async_copy(source, target, sems.at[i]) for i, (source, target) in enumerate(pairs)]
    for copy in copies:
        copy.start()
    for copy in copies:
        copy.wait()


def join_kernel(*refs):
    parts, (column_ref, ends_ref, sems) = refs[:-3], refs[-3:]
    pairs = []
    for out_ref, sources in ((column_ref, parts[:4]), (ends_ref, parts[4:])):
        start = 0
        for ref in sources:
            pairs.append((ref, out_ref.at[start : start + ref.shape[0], :]))
            start += ref.shape[0]
    run_copies(pairs, sems)


def join(column, ends):
    width = column[0].shape[1]
    heights = [sum(part.shape[0] for part in parts) for parts in (column, ends)]
    return pl.pallas_call(
        join_kernel,
        grid=(1,),
        in_specs=[HBM] * 6,
        out_specs=[pl.BlockSpec((rows, width), lambda i: (0, 0)) for rows in heights],
        out_shape=[jax.ShapeDtypeStruct((rows, width), column[0].dtype) for rows in heights],
        scratch_shapes=[pltpu.SemaphoreType.DMA((6,))],
        compiler_params=pltpu.CompilerParams(vmem_limit_bytes=PAIR_VMEM_BYTES),
        name="join",
    )(*column, *ends)


def text_index(place_ref, texts):
    lane = lax.broadcasted_iota(jnp.int32, (1, texts), 1)
    column, part, row = lane >> 8, (lane >> 6) & 3, lane & 63
    dx = jnp.where(column == 1, -1, column - (column >> 1))
    far = jnp.where(row < 32, -2, 2)
    dz = jnp.where(part == 3, far, jnp.where(part == 2, 1, -part))
    z = (place_ref[0] + dz) & 7
    x = (place_ref[2] + dx) & 3
    device = (z >> 2) * 128 + place_ref[1] * 32 + x * 8 + (z & 3) * 2 + place_ref[3]
    return device * 64 + row


def pair_block(scal_ref, image, text, row_ids, text_ids, stat_ref):
    products = lax.dot_general(image, text, (((1,), (1,)), ((), ())), preferred_element_type=jnp.float32)
    logits = scal_ref[0] * products + scal_ref[1]
    paired = row_ids == text_ids
    grown = jnp.exp(logits)
    above = 1.0 + grown
    coeff = jnp.where(paired, -1.0, grown) * pl.reciprocal(above)
    loss = jnp.where(grown < 1e-3, grown * (1.0 - 0.5 * grown), jnp.log(above))
    loss = loss - jnp.where(paired, logits, 0.0)
    width = products.shape[1]
    stat_ref[0] += jnp.sum(loss.reshape(-1, 8, width), axis=0)
    stat_ref[1] += jnp.sum((coeff * products).reshape(-1, 8, width), axis=0)
    stat_ref[2] += jnp.sum(coeff.reshape(-1, 8, width), axis=0)
    return coeff.astype(jnp.bfloat16)


def pair_kernel(side, scal_ref, place_ref, image_ref, *rest):
    if side == 0:
        pieces, rest = rest[:7], rest[7:]
        grad_ref, coef_ref, copy_ref, text_ref, stat_ref, sems = rest
    else:
        text_ref, sums_ref, _, _, grad_ref, coef_ref, copy_ref, total_ref, stat_ref, sems = rest
    count = image_ref.shape[0]
    quarter = count // 4
    columns = coef_ref.shape[2]
    block = columns // 4
    starts = [pl.multiple_of(((place_ref[1] + dy) & 3) * quarter, quarter) for dy in (0, 1, 3, 2)]
    pairs = [
        (image_ref.at[pl.ds(start, quarter), :], copy_ref.at[i * quarter : (i + 1) * quarter, :])
        for i, start in enumerate(starts)
    ]
    if side == 0:
        for k in range(4):
            for j in range(4):
                piece = pieces[j].at[block * k : block * (k + 1), :] if j < 3 else pieces[3 + k]
                at = columns * k + block * j
                pairs.append((piece, text_ref.at[at : at + block, :]))
    run_copies(pairs, sems)
    stat_ref[...] = jnp.zeros_like(stat_ref) if side == 0 else sums_ref[...]
    text = text_ref[...]
    ids = text_index(place_ref, text.shape[0])
    row_iota = lax.broadcasted_iota(jnp.int32, (quarter, 1), 0) + place_ref[4 + side]
    for half in range(2):
        rows = slice(2 * half * quarter, 2 * (half + 1) * quarter)
        row_ids = jnp.concatenate([row_iota + start for start in starts[2 * half : 2 * half + 2]])
        coeff = pair_block(scal_ref, copy_ref[rows, :], text, row_ids, ids, stat_ref)
        grad_ref[rows, :] = jnp.dot(coeff, text, preferred_element_type=jnp.float32)
        for k in range(4):
            coef_ref[k, rows, :] = coeff[:, k * columns : (k + 1) * columns]
    if side == 1:
        total_ref[...] = jnp.zeros_like(total_ref)
        for k in range(3):
            stat = stat_ref[k]
            lanes = sum(stat[:, 128 * i : 128 * (i + 1)] for i in range(stat.shape[1] // 128))
            total_ref[k : k + 1, :] = jnp.sum(lanes, axis=0, keepdims=True)


def pair_terms(scalars, place, other, own, col, below, above, far):
    count, width = own.shape
    texts = 4 * col.shape[0]
    f32, bf16 = jnp.float32, jnp.bfloat16
    shape = jax.ShapeDtypeStruct
    cost = pl.CostEstimate(
        flops=4 * count * texts * width, bytes_accessed=12 * count * width, transcendentals=3 * count * texts
    )
    params = pltpu.CompilerParams(vmem_limit_bytes=PAIR_VMEM_BYTES)
    whole = lambda *dims: pl.BlockSpec(dims, lambda i: (0,) * len(dims))
    coef_shape, copy_shape = shape((4, 2 * count, texts // 4), bf16), shape((2 * count, width), bf16)
    stat = (3, 8, texts)
    grad_other, coef, copies, text, sums = pl.pallas_call(
        lambda *refs: pair_kernel(0, *refs),
        grid=(1,),
        in_specs=[SMEM, SMEM] + [HBM] * 8,
        out_specs=[
            whole(count, width),
            whole(4, count, texts // 4),
            whole(count, width),
            whole(texts, width),
            whole(*stat),
        ],
        out_shape=[shape((count, width), f32), coef_shape, copy_shape, shape((texts, width), bf16), shape(stat, f32)],
        scratch_shapes=[pltpu.SemaphoreType.DMA((20,))],
        compiler_params=params,
        cost_estimate=cost,
        name="other_rows",
    )(scalars, place, other, col, below, above, *far)
    grad_own, coef, copies, total = pl.pallas_call(
        lambda *refs: pair_kernel(1, *refs),
        grid=(1,),
        in_specs=[SMEM, SMEM, HBM, whole(texts, width), whole(*stat), HBM, HBM],
        out_specs=[
            whole(count, width),
            pl.BlockSpec((4, count, texts // 4), lambda i: (0, 1, 0)),
            pl.BlockSpec((count, width), lambda i: (1, 0)),
            whole(8, 128),
        ],
        out_shape=[shape((count, width), f32), coef_shape, copy_shape, shape((8, 128), f32)],
        scratch_shapes=[pltpu.VMEM(stat, f32), pltpu.SemaphoreType.DMA((4,))],
        input_output_aliases={5: 1, 6: 2},
        compiler_params=params,
        cost_estimate=cost,
        name="own_rows",
    )(scalars, place, own, text, sums, coef, copies)
    return grad_other, grad_own, coef, copies, total


def per_device(picture_embeddings, caption_embeddings, exponent_of_sharpness, offset_shift):
    count, width = picture_embeddings.shape
    group, blk = lax.axis_index("group"), lax.axis_index("blk")
    z, y, x, core = (group // 4) * 4 + (blk // 2) % 4, group % 4, blk // 8, blk % 2
    temperature = jnp.exp(exponent_of_sharpness[0])
    scalars = jnp.stack([temperature, offset_shift[0]])
    place = jnp.stack([z, y, x, core, (blk ^ 1) * count, blk * count]).astype(jnp.int32)

    text_rows, text_a, text_b = text_messages(caption_embeddings)
    pictures, text_rows = lax.optimization_barrier((picture_embeddings, text_rows))
    column, ends = join(
        (text_rows, move(text_rows, dx=1), move(text_rows, dx=-1), move(text_rows, dx=2)),
        (move(text_a, dz=2), move(text_b, dz=-2)),
    )
    unit_image, inv_image = normalize_rows(pictures)
    image_rows = unit_image.astype(jnp.bfloat16)
    other_rows = move(image_rows, swap=1)
    below, above = move(column, dz=1), move(column, dz=-1)
    far = [ends, move(ends, dx=1), move(ends, dx=-1), move(ends, dx=2)]

    grad_other, grad_own, coef, copies, total = pair_terms(
        scalars, place, other_rows, image_rows, column, below, above, far
    )

    quarter = count // 4
    received = move(grad_other, swap=1)
    parts = [
        (grad_own[k * quarter : (k + 1) * quarter] + received[k * quarter : (k + 1) * quarter]).astype(SEND)
        for k in range(4)
    ]
    arrived = [move(parts[1], dy=1), move(parts[2], dy=-1), move(parts[3], dy=2)]

    coef, copies, parts[0] = lax.optimization_barrier((coef, copies, parts[0]))
    blocks = [
        lax.dot_general(coef[k], copies, (((0,), (0,)), ((), ())), preferred_element_type=jnp.float32).astype(SEND)
        for k in range(4)
    ]
    x_terms = [blocks[0], move(blocks[1], dx=-1), move(blocks[2], dx=1), move(blocks[3], dx=2)]

    y_sum = sum(part.astype(jnp.float32) for part in [parts[0]] + arrived).astype(SEND)
    image_grad = y_sum.astype(jnp.float32) + move(y_sum, dz=4).astype(jnp.float32)
    unit_part = lax.dynamic_slice_in_dim(unit_image, y * quarter, quarter)
    tangent = (image_grad - unit_part * jnp.sum(unit_part * image_grad, axis=1, keepdims=True)).astype(SEND)
    tangents = [tangent] + [move(tangent, dy=dy) for dy in (1, -1, 2)]

    n = caption_embeddings.shape[0]
    h = n // 2
    *x_terms, tangent = lax.optimization_barrier((*x_terms, tangent))
    x_sum = sum(term.astype(jnp.float32) for term in x_terms).astype(SEND)
    near = [move(x_sum[n : 2 * n], dz=-1), move(x_sum[2 * n : 3 * n], dz=1)]
    ends_sum = [move(x_sum[3 * n : 3 * n + h], dz=-2), move(x_sum[3 * n + h :], dz=2)]
    *tangents, near[0], near[1], ends_sum[0], ends_sum[1] = lax.optimization_barrier((*tangents, *near, *ends_sum))

    slope = jnp.zeros((count, width), SEND)
    for dy, got in zip((0, 1, -1, 2), tangents):
        slope = lax.dynamic_update_slice_in_dim(slope, got, ((y - dy) % 4) * quarter, 0)
    picture_embedding_slope = slope.astype(jnp.float32) * (temperature * inv_image)

    text_sum = x_sum[:n].astype(jnp.float32) + jnp.concatenate(ends_sum).astype(jnp.float32)
    text_sum += near[0].astype(jnp.float32) + near[1].astype(jnp.float32)
    unit_text, inv_text = normalize_rows(caption_embeddings)
    text_grad = (text_sum - unit_text * jnp.sum(unit_text * text_sum, axis=1, keepdims=True)) * (
        temperature * inv_text
    )

    for done, bits in ((parts[0], (0, 3, 4)), (y_sum, (5, 6)), (tangent, (1, 2, 7))):
        total, _ = lax.optimization_barrier((total, done))
        for bit in bits:
            total += lax.ppermute(total, AXES, [(i, i ^ (1 << bit)) for i in range(256)])
    total = jnp.sum(total, axis=1)
    rows_overall = count * lax.axis_size("blk")
    statistics = jnp.stack([total[0], temperature * total[1], total[2]]) / rows_overall
    return (picture_embedding_slope, text_grad, statistics)


def solution(mesh):
    placed = (P("blk", None), P(("group", "blk"), None), P(), P())
    return jax.shard_map(
        per_device,
        mesh=mesh,
        in_specs=placed,
        out_specs=(P("blk", None), P(("group", "blk"), None), P()),
        check_vma=False,
    )
```

```python
import jax
import jax.numpy as jnp
from jax import lax
from jax.experimental import pallas as pl
from jax.experimental.pallas import tpu as pltpu
from jax.sharding import PartitionSpec as P

AXES = ("group", "blk")
SEND = jnp.float16
STAT_SCALE = 2.0**-14
VMEM_BYTES = 58 * 1024 * 1024
PAIR_VMEM_BYTES = 44 * 1024 * 1024
SMEM = pl.BlockSpec(memory_space=pltpu.SMEM)
HBM = pl.BlockSpec(memory_space=pltpu.HBM)


def device_index(z, y, x, core):
    return (((z // 4) * 4 + y) * 4 + x) * 8 + (z % 4) * 2 + core


def shifted(dz=0, dy=0, dx=0, swap=0):
    pairs = []
    for z in range(8):
        for y in range(4):
            for x in range(4):
                for core in range(2):
                    there = device_index((z + dz) % 8, (y + dy) % 4, (x + dx) % 4, core ^ swap)
                    pairs.append((device_index(z, y, x, core), there))
    return pairs


def move(value, **shift):
    return lax.ppermute(value, AXES, shifted(**shift))


def sums_rows(total, width):
    high = lax.optimization_barrier(total.astype(SEND))
    low = (total - high.astype(jnp.float32)).astype(SEND)
    sums = jnp.pad(jnp.concatenate([high, low]), ((0, 0), (0, width - total.shape[1])))
    return lax.optimization_barrier(sums)


def ring_sum(own, ahead, behind, far):
    return (own + far) + (ahead + behind)


def sums_of(message):
    high, low = message[-8:-4, :128], message[-4:, :128]
    return high.astype(jnp.float32) + low.astype(jnp.float32)


def normalize_rows(matrix):
    inverse_norm = lax.rsqrt(jnp.sum(matrix * matrix, axis=1, keepdims=True) + 1e-06)
    return (matrix * inverse_norm, inverse_norm)


def text_kernel(text_ref, rows_ref, a_ref, b_ref):
    text = text_ref[...]
    rows = (text * lax.rsqrt(jnp.sum(text * text, axis=1, keepdims=True) + 1e-06)).astype(jnp.bfloat16)
    half = a_ref.shape[0]
    rows_ref[...] = rows
    a_ref[...] = rows[:half]
    b_ref[...] = rows[half:]


def text_messages(texts):
    n, width = texts.shape
    shape = lambda rows: jax.ShapeDtypeStruct((rows, width), jnp.bfloat16)
    return pl.pallas_call(
        text_kernel,
        grid=(1,),
        in_specs=[pl.BlockSpec((n, width), lambda i: (0, 0))],
        out_specs=[pl.BlockSpec((rows, width), lambda i: (0, 0)) for rows in (n, n // 2, n // 2)],
        out_shape=[shape(n), shape(n // 2), shape(n // 2)],
        compiler_params=pltpu.CompilerParams(vmem_limit_bytes=VMEM_BYTES),
        name="text_rows",
    )(texts)


def run_copies(pairs, sems):
    copies = [pltpu.make_async_copy(source, target, sems.at[i]) for i, (source, target) in enumerate(pairs)]
    for copy in copies:
        copy.start()
    for copy in copies:
        copy.wait()


def join_kernel(*refs):
    parts, (column_ref, ends_ref, sems) = refs[:-3], refs[-3:]
    pairs = []
    for out_ref, sources in ((column_ref, parts[:4]), (ends_ref, parts[4:])):
        start = 0
        for ref in sources:
            pairs.append((ref, out_ref.at[start : start + ref.shape[0], :]))
            start += ref.shape[0]
    run_copies(pairs, sems)


def join(column, ends):
    width = column[0].shape[1]
    heights = [sum(part.shape[0] for part in parts) for parts in (column, ends)]
    return pl.pallas_call(
        join_kernel,
        grid=(1,),
        in_specs=[HBM] * 6,
        out_specs=[pl.BlockSpec((rows, width), lambda i: (0, 0)) for rows in heights],
        out_shape=[jax.ShapeDtypeStruct((rows, width), column[0].dtype) for rows in heights],
        scratch_shapes=[pltpu.SemaphoreType.DMA((6,))],
        compiler_params=pltpu.CompilerParams(vmem_limit_bytes=PAIR_VMEM_BYTES),
        name="join",
    )(*column, *ends)


def text_index(place_ref, texts):
    lane = lax.broadcasted_iota(jnp.int32, (1, texts), 1)
    column, part, row = lane >> 8, (lane >> 6) & 3, lane & 63
    dx = jnp.where(column == 1, -1, column - (column >> 1))
    far = jnp.where(row < 32, -2, 2)
    dz = jnp.where(part == 3, far, jnp.where(part == 2, 1, -part))
    z = (place_ref[0] + dz) & 7
    x = (place_ref[2] + dx) & 3
    device = (z >> 2) * 128 + place_ref[1] * 32 + x * 8 + (z & 3) * 2 + place_ref[3]
    return device * 64 + row


def pair_block(scal_ref, image, text, row_ids, text_ids, stat_ref):
    products = lax.dot_general(image, text, (((1,), (1,)), ((), ())), preferred_element_type=jnp.float32)
    logits = scal_ref[0] * products + scal_ref[1]
    paired = row_ids == text_ids
    grown = jnp.exp(logits)
    above = 1.0 + grown
    coeff = jnp.where(paired, -1.0, grown) * pl.reciprocal(above)
    loss = jnp.where(grown < 1e-3, grown * (1.0 - 0.5 * grown), jnp.log(above))
    loss = loss - jnp.where(paired, logits, 0.0)
    width = products.shape[1]
    stat_ref[0] += jnp.sum(loss.reshape(-1, 8, width), axis=0)
    stat_ref[1] += jnp.sum((coeff * products).reshape(-1, 8, width), axis=0)
    stat_ref[2] += jnp.sum(coeff.reshape(-1, 8, width), axis=0)
    return coeff.astype(jnp.bfloat16)


def pair_kernel(side, scal_ref, place_ref, image_ref, *rest):
    if side == 0:
        pieces, rest = rest[:7], rest[7:]
        grad_ref, coef_ref, copy_ref, text_ref, stat_ref, sems = rest
    else:
        text_ref, sums_ref, _, _, grad_ref, coef_ref, copy_ref, total_ref, stat_ref, sems = rest
    count = image_ref.shape[0]
    quarter = count // 4
    columns = coef_ref.shape[2]
    block = columns // 4
    starts = [pl.multiple_of(((place_ref[1] + dy) & 3) * quarter, quarter) for dy in (0, 1, 3, 2)]
    pairs = [
        (image_ref.at[pl.ds(start, quarter), :], copy_ref.at[i * quarter : (i + 1) * quarter, :])
        for i, start in enumerate(starts)
    ]
    if side == 0:
        for k in range(4):
            for j in range(4):
                piece = pieces[j].at[block * k : block * (k + 1), :] if j < 3 else pieces[3 + k]
                at = columns * k + block * j
                pairs.append((piece, text_ref.at[at : at + block, :]))
    run_copies(pairs, sems)
    stat_ref[...] = jnp.zeros_like(stat_ref) if side == 0 else sums_ref[...]
    text = text_ref[...]
    ids = text_index(place_ref, text.shape[0])
    row_iota = lax.broadcasted_iota(jnp.int32, (quarter, 1), 0) + place_ref[4 + side]
    for half in range(2):
        rows = slice(2 * half * quarter, 2 * (half + 1) * quarter)
        row_ids = jnp.concatenate([row_iota + start for start in starts[2 * half : 2 * half + 2]])
        coeff = pair_block(scal_ref, copy_ref[rows, :], text, row_ids, ids, stat_ref)
        grad_ref[rows, :] = jnp.dot(coeff, text, preferred_element_type=jnp.float32)
        for k in range(4):
            coef_ref[k, rows, :] = coeff[:, k * columns : (k + 1) * columns]
    if side == 1:
        total_ref[...] = jnp.zeros_like(total_ref)
        for k in range(3):
            stat = stat_ref[k]
            lanes = sum(stat[:, 128 * i : 128 * (i + 1)] for i in range(stat.shape[1] // 128))
            each = jnp.sum(jnp.sum(lanes, axis=0, keepdims=True), axis=1, keepdims=True)
            total_ref[k : k + 1, :] = jnp.broadcast_to(each * STAT_SCALE, (1, 128))


def pair_terms(scalars, place, other, own, col, below, above, far):
    count, width = own.shape
    texts = 4 * col.shape[0]
    f32, bf16 = jnp.float32, jnp.bfloat16
    shape = jax.ShapeDtypeStruct
    cost = pl.CostEstimate(
        flops=4 * count * texts * width, bytes_accessed=12 * count * width, transcendentals=3 * count * texts
    )
    params = pltpu.CompilerParams(vmem_limit_bytes=PAIR_VMEM_BYTES)
    whole = lambda *dims: pl.BlockSpec(dims, lambda i: (0,) * len(dims))
    coef_shape, copy_shape = shape((4, 2 * count, texts // 4), bf16), shape((2 * count, width), bf16)
    stat = (3, 8, texts)
    grad_other, coef, copies, text, sums = pl.pallas_call(
        lambda *refs: pair_kernel(0, *refs),
        grid=(1,),
        in_specs=[SMEM, SMEM] + [HBM] * 8,
        out_specs=[
            whole(count, width),
            whole(4, count, texts // 4),
            whole(count, width),
            whole(texts, width),
            whole(*stat),
        ],
        out_shape=[shape((count, width), f32), coef_shape, copy_shape, shape((texts, width), bf16), shape(stat, f32)],
        scratch_shapes=[pltpu.SemaphoreType.DMA((20,))],
        compiler_params=params,
        cost_estimate=cost,
        name="other_rows",
    )(scalars, place, other, col, below, above, *far)
    grad_own, coef, copies, total = pl.pallas_call(
        lambda *refs: pair_kernel(1, *refs),
        grid=(1,),
        in_specs=[SMEM, SMEM, HBM, whole(texts, width), whole(*stat), HBM, HBM],
        out_specs=[
            whole(count, width),
            pl.BlockSpec((4, count, texts // 4), lambda i: (0, 1, 0)),
            pl.BlockSpec((count, width), lambda i: (1, 0)),
            whole(8, 128),
        ],
        out_shape=[shape((count, width), f32), coef_shape, copy_shape, shape((8, 128), f32)],
        scratch_shapes=[pltpu.VMEM(stat, f32), pltpu.SemaphoreType.DMA((4,))],
        input_output_aliases={5: 1, 6: 2},
        compiler_params=params,
        cost_estimate=cost,
        name="own_rows",
    )(scalars, place, own, text, sums, coef, copies)
    return grad_other, grad_own, coef, copies, total


def per_device(picture_embeddings, caption_embeddings, exponent_of_sharpness, offset_shift):
    count, width = picture_embeddings.shape
    group, blk = lax.axis_index("group"), lax.axis_index("blk")
    z, y, x, core = (group // 4) * 4 + (blk // 2) % 4, group % 4, blk // 8, blk % 2
    temperature = jnp.exp(exponent_of_sharpness[0])
    scalars = jnp.stack([temperature, offset_shift[0]])
    place = jnp.stack([z, y, x, core, (blk ^ 1) * count, blk * count]).astype(jnp.int32)

    text_rows, text_a, text_b = text_messages(caption_embeddings)
    pictures, text_rows = lax.optimization_barrier((picture_embeddings, text_rows))
    column, ends = join(
        (text_rows, move(text_rows, dx=1), move(text_rows, dx=-1), move(text_rows, dx=2)),
        (move(text_a, dz=2), move(text_b, dz=-2)),
    )
    unit_image, inv_image = normalize_rows(pictures)
    image_rows = unit_image.astype(jnp.bfloat16)
    other_rows = move(image_rows, swap=1)
    below, above = move(column, dz=1), move(column, dz=-1)
    far = [ends, move(ends, dx=1), move(ends, dx=-1), move(ends, dx=2)]

    grad_other, grad_own, coef, copies, total = pair_terms(
        scalars, place, other_rows, image_rows, column, below, above, far
    )

    quarter = count // 4
    received = move(grad_other, swap=1)
    parts = [
        (grad_own[k * quarter : (k + 1) * quarter] + received[k * quarter : (k + 1) * quarter]).astype(SEND)
        for k in range(4)
    ]
    total = total[:4]
    for bit in (0, 3, 4):
        total += lax.ppermute(total, AXES, [(i, i ^ (1 << bit)) for i in range(256)])
    own_sums = sums_rows(total, width)
    arrived = [move(jnp.concatenate([part, own_sums]), dy=dy) for part, dy in zip(parts[1:], (1, -1, 2))]

    coef, copies, parts[0] = lax.optimization_barrier((coef, copies, parts[0]))
    blocks = [
        lax.dot_general(coef[k], copies, (((0,), (0,)), ((), ())), preferred_element_type=jnp.float32).astype(SEND)
        for k in range(4)
    ]
    x_terms = [blocks[0], move(blocks[1], dx=-1), move(blocks[2], dx=1), move(blocks[3], dx=2)]

    y_sum = sum(part[:quarter].astype(jnp.float32) for part in [parts[0]] + arrived).astype(SEND)
    total = ring_sum(sums_of(own_sums), *[sums_of(message) for message in arrived])
    y_sum = lax.optimization_barrier(jnp.concatenate([y_sum, sums_rows(total, width)]))
    z_sum = move(y_sum, dz=4)
    total = sums_of(y_sum) + sums_of(z_sum)
    image_grad = y_sum[:quarter].astype(jnp.float32) + z_sum[:quarter].astype(jnp.float32)
    unit_part = lax.dynamic_slice_in_dim(unit_image, y * quarter, quarter)
    tangent = (image_grad - unit_part * jnp.sum(unit_part * image_grad, axis=1, keepdims=True)).astype(SEND)
    tangent = lax.optimization_barrier(tangent)
    tangents = [tangent] + [move(tangent, dy=dy) for dy in (1, -1, 2)]

    n = caption_embeddings.shape[0]
    h = n // 2
    *x_terms, tangents[1] = lax.optimization_barrier((*x_terms, tangents[1]))
    x_sum = sum(term.astype(jnp.float32) for term in x_terms).astype(SEND)
    own_sums = sums_rows(total, width)
    ride = lambda rows: jnp.concatenate([rows, own_sums])
    near = [move(ride(x_sum[n : 2 * n]), dz=-1), move(ride(x_sum[2 * n : 3 * n]), dz=1)]
    ends_sum = [move(ride(x_sum[3 * n : 3 * n + h]), dz=-2), move(x_sum[3 * n + h :], dz=2)]

    slope = jnp.zeros((count, width), SEND)
    for dy, got in zip((0, 1, -1, 2), tangents):
        slope = lax.dynamic_update_slice_in_dim(slope, got, ((y - dy) % 4) * quarter, 0)
    picture_embedding_slope = slope.astype(jnp.float32) * (temperature * inv_image)
    picture_embedding_slope, near[0], near[1], ends_sum[0], ends_sum[1] = lax.optimization_barrier(
        (picture_embedding_slope, *near, *ends_sum)
    )

    total = ring_sum(*[sums_of(message) for message in (own_sums, near[0], near[1], ends_sum[0])])
    text_sum = x_sum[:n].astype(jnp.float32) + jnp.concatenate([ends_sum[0][:h], ends_sum[1]]).astype(jnp.float32)
    text_sum += near[0][:n].astype(jnp.float32) + near[1][:n].astype(jnp.float32)
    unit_text, inv_text = normalize_rows(caption_embeddings)
    text_grad = (text_sum - unit_text * jnp.sum(unit_text * text_sum, axis=1, keepdims=True)) * (
        temperature * inv_text
    )

    rows_overall = count * lax.axis_size("blk")
    scale = jnp.where(jnp.arange(3) == 1, temperature, 1.0) / (STAT_SCALE * rows_overall)
    statistics = total[:3, 0] * scale
    return (picture_embedding_slope, text_grad, statistics)


def solution(mesh):
    placed = (P("blk", None), P(("group", "blk"), None), P(), P())
    return jax.shard_map(
        per_device,
        mesh=mesh,
        in_specs=placed,
        out_specs=(P("blk", None), P(("group", "blk"), None), P()),
        check_vma=False,
    )
```

```python
import jax
import jax.numpy as jnp
from jax import lax
from jax.experimental import pallas as pl
from jax.experimental.pallas import tpu as pltpu
from jax.sharding import PartitionSpec as P

AXES = ("group", "blk")
SEND = jnp.float16
STAT_SCALE = 2.0**-14
VMEM_BYTES = 28 * 1024 * 1024
PAIR_VMEM_BYTES = 28 * 1024 * 1024
SMEM = pl.BlockSpec(memory_space=pltpu.SMEM)
HBM = pl.BlockSpec(memory_space=pltpu.HBM)


def device_index(z, y, x, core):
    return (((z // 4) * 4 + y) * 4 + x) * 8 + (z % 4) * 2 + core


def shifted(dz=0, dy=0, dx=0, swap=0):
    pairs = []
    for z in range(8):
        for y in range(4):
            for x in range(4):
                for core in range(2):
                    there = device_index((z + dz) % 8, (y + dy) % 4, (x + dx) % 4, core ^ swap)
                    pairs.append((device_index(z, y, x, core), there))
    return pairs


def move(value, **shift):
    return lax.ppermute(value, AXES, shifted(**shift))


def sums_rows(total, width):
    high = lax.optimization_barrier(total.astype(SEND))
    low = (total - high.astype(jnp.float32)).astype(SEND)
    sums = jnp.pad(jnp.concatenate([high, low]), ((0, 0), (0, width - total.shape[1])))
    return lax.optimization_barrier(sums)


def ring_sum(own, ahead, behind, far):
    return (own + far) + (ahead + behind)


def sums_of(message):
    high, low = message[-8:-4, :128], message[-4:, :128]
    return high.astype(jnp.float32) + low.astype(jnp.float32)


def normalize_rows(matrix):
    inverse_norm = lax.rsqrt(jnp.sum(matrix * matrix, axis=1, keepdims=True) + 1e-06)
    return (matrix * inverse_norm, inverse_norm)


def text_kernel(text_ref, rows_ref, a_ref, b_ref):
    text = text_ref[...]
    rows = (text * lax.rsqrt(jnp.sum(text * text, axis=1, keepdims=True) + 1e-06)).astype(jnp.bfloat16)
    half = a_ref.shape[0]
    rows_ref[...] = rows
    a_ref[...] = rows[:half]
    b_ref[...] = rows[half:]


def text_messages(texts):
    n, width = texts.shape
    shape = lambda rows: jax.ShapeDtypeStruct((rows, width), jnp.bfloat16)
    return pl.pallas_call(
        text_kernel,
        grid=(1,),
        in_specs=[pl.BlockSpec((n, width), lambda i: (0, 0))],
        out_specs=[pl.BlockSpec((rows, width), lambda i: (0, 0)) for rows in (n, n // 2, n // 2)],
        out_shape=[shape(n), shape(n // 2), shape(n // 2)],
        compiler_params=pltpu.CompilerParams(vmem_limit_bytes=VMEM_BYTES),
        name="text_rows",
    )(texts)


def run_copies(pairs, sems):
    copies = [pltpu.make_async_copy(source, target, sems.at[i]) for i, (source, target) in enumerate(pairs)]
    for copy in copies:
        copy.start()
    for copy in copies:
        copy.wait()


def join_kernel(*refs):
    parts, (column_ref, ends_ref, sems) = refs[:-3], refs[-3:]
    pairs = []
    for out_ref, sources in ((column_ref, parts[:4]), (ends_ref, parts[4:])):
        start = 0
        for ref in sources:
            pairs.append((ref, out_ref.at[start : start + ref.shape[0], :]))
            start += ref.shape[0]
    run_copies(pairs, sems)


def join(column, ends):
    width = column[0].shape[1]
    heights = [sum(part.shape[0] for part in parts) for parts in (column, ends)]
    return pl.pallas_call(
        join_kernel,
        grid=(1,),
        in_specs=[HBM] * 6,
        out_specs=[pl.BlockSpec((rows, width), lambda i: (0, 0)) for rows in heights],
        out_shape=[jax.ShapeDtypeStruct((rows, width), column[0].dtype) for rows in heights],
        scratch_shapes=[pltpu.SemaphoreType.DMA((6,))],
        compiler_params=pltpu.CompilerParams(vmem_limit_bytes=PAIR_VMEM_BYTES),
        name="join",
    )(*column, *ends)


def text_index(place_ref, texts):
    lane = lax.broadcasted_iota(jnp.int32, (1, texts), 1)
    column, part, row = lane >> 8, (lane >> 6) & 3, lane & 63
    dx = jnp.where(column == 1, -1, column - (column >> 1))
    far = jnp.where(row < 32, -2, 2)
    dz = jnp.where(part == 3, far, jnp.where(part == 2, 1, -part))
    z = (place_ref[0] + dz) & 7
    x = (place_ref[2] + dx) & 3
    device = (z >> 2) * 128 + place_ref[1] * 32 + x * 8 + (z & 3) * 2 + place_ref[3]
    return device * 64 + row


def pair_block(scal_ref, image, text, row_ids, text_ids, stat_ref):
    products = lax.dot_general(image, text, (((1,), (1,)), ((), ())), preferred_element_type=jnp.float32)
    logits = scal_ref[0] * products + scal_ref[1]
    paired = row_ids == text_ids
    grown = jnp.exp(logits)
    above = 1.0 + grown
    coeff = jnp.where(paired, -1.0, grown) * pl.reciprocal(above)
    loss = jnp.where(grown < 1e-3, grown * (1.0 - 0.5 * grown), jnp.log(above))
    loss = loss - jnp.where(paired, logits, 0.0)
    width = products.shape[1]
    stat_ref[0] += jnp.sum(loss.reshape(-1, 8, width), axis=0)
    stat_ref[1] += jnp.sum((coeff * products).reshape(-1, 8, width), axis=0)
    stat_ref[2] += jnp.sum(coeff.reshape(-1, 8, width), axis=0)
    return coeff.astype(jnp.bfloat16)


def pair_kernel(side, scal_ref, place_ref, image_ref, *rest):
    if side == 0:
        pieces, rest = rest[:7], rest[7:]
        grad_ref, coef_ref, copy_ref, text_ref, stat_ref, sems = rest
    else:
        text_ref, sums_ref, _, _, grad_ref, coef_ref, copy_ref, total_ref, stat_ref, sems = rest
    count = image_ref.shape[0]
    quarter = count // 4
    columns = coef_ref.shape[2]
    block = columns // 4
    starts = [pl.multiple_of(((place_ref[1] + dy) & 3) * quarter, quarter) for dy in (0, 1, 3, 2)]
    pairs = [
        (image_ref.at[pl.ds(start, quarter), :], copy_ref.at[i * quarter : (i + 1) * quarter, :])
        for i, start in enumerate(starts)
    ]
    if side == 0:
        for k in range(4):
            for j in range(4):
                piece = pieces[j].at[block * k : block * (k + 1), :] if j < 3 else pieces[3 + k]
                at = columns * k + block * j
                pairs.append((piece, text_ref.at[at : at + block, :]))
    run_copies(pairs, sems)
    stat_ref[...] = jnp.zeros_like(stat_ref) if side == 0 else sums_ref[...]
    text = text_ref[...]
    ids = text_index(place_ref, text.shape[0])
    row_iota = lax.broadcasted_iota(jnp.int32, (quarter, 1), 0) + place_ref[4 + side]
    for half in range(2):
        rows = slice(2 * half * quarter, 2 * (half + 1) * quarter)
        row_ids = jnp.concatenate([row_iota + start for start in starts[2 * half : 2 * half + 2]])
        coeff = pair_block(scal_ref, copy_ref[rows, :], text, row_ids, ids, stat_ref)
        grad_ref[rows, :] = jnp.dot(coeff, text, preferred_element_type=jnp.float32)
        for k in range(4):
            coef_ref[k, rows, :] = coeff[:, k * columns : (k + 1) * columns]
    if side == 1:
        total_ref[...] = jnp.zeros_like(total_ref)
        for k in range(3):
            stat = stat_ref[k]
            lanes = sum(stat[:, 128 * i : 128 * (i + 1)] for i in range(stat.shape[1] // 128))
            each = jnp.sum(jnp.sum(lanes, axis=0, keepdims=True), axis=1, keepdims=True)
            total_ref[k : k + 1, :] = jnp.broadcast_to(each * STAT_SCALE, (1, 128))


def pair_terms(scalars, place, other, own, col, below, above, far):
    count, width = own.shape
    texts = 4 * col.shape[0]
    f32, bf16 = jnp.float32, jnp.bfloat16
    shape = jax.ShapeDtypeStruct
    cost = pl.CostEstimate(
        flops=4 * count * texts * width, bytes_accessed=12 * count * width, transcendentals=3 * count * texts
    )
    params = pltpu.CompilerParams(vmem_limit_bytes=PAIR_VMEM_BYTES)
    whole = lambda *dims: pl.BlockSpec(dims, lambda i: (0,) * len(dims))
    coef_shape, copy_shape = shape((4, 2 * count, texts // 4), bf16), shape((2 * count, width), bf16)
    stat = (3, 8, texts)
    grad_other, coef, copies, text, sums = pl.pallas_call(
        lambda *refs: pair_kernel(0, *refs),
        grid=(1,),
        in_specs=[SMEM, SMEM] + [HBM] * 8,
        out_specs=[
            whole(count, width),
            whole(4, count, texts // 4),
            whole(count, width),
            whole(texts, width),
            whole(*stat),
        ],
        out_shape=[shape((count, width), f32), coef_shape, copy_shape, shape((texts, width), bf16), shape(stat, f32)],
        scratch_shapes=[pltpu.SemaphoreType.DMA((20,))],
        compiler_params=params,
        cost_estimate=cost,
        name="other_rows",
    )(scalars, place, other, col, below, above, *far)
    grad_own, coef, copies, total = pl.pallas_call(
        lambda *refs: pair_kernel(1, *refs),
        grid=(1,),
        in_specs=[SMEM, SMEM, HBM, whole(texts, width), whole(*stat), HBM, HBM],
        out_specs=[
            whole(count, width),
            pl.BlockSpec((4, count, texts // 4), lambda i: (0, 1, 0)),
            pl.BlockSpec((count, width), lambda i: (1, 0)),
            whole(8, 128),
        ],
        out_shape=[shape((count, width), f32), coef_shape, copy_shape, shape((8, 128), f32)],
        scratch_shapes=[pltpu.VMEM(stat, f32), pltpu.SemaphoreType.DMA((4,))],
        input_output_aliases={5: 1, 6: 2},
        compiler_params=params,
        cost_estimate=cost,
        name="own_rows",
    )(scalars, place, own, text, sums, coef, copies)
    return grad_other, grad_own, coef, copies, total


def per_device(picture_embeddings, caption_embeddings, exponent_of_sharpness, offset_shift):
    count, width = picture_embeddings.shape
    group, blk = lax.axis_index("group"), lax.axis_index("blk")
    z, y, x, core = (group // 4) * 4 + (blk // 2) % 4, group % 4, blk // 8, blk % 2
    temperature = jnp.exp(exponent_of_sharpness[0])
    scalars = jnp.stack([temperature, offset_shift[0]])
    place = jnp.stack([z, y, x, core, (blk ^ 1) * count, blk * count]).astype(jnp.int32)

    text_rows, text_a, text_b = text_messages(caption_embeddings)
    pictures, text_rows = lax.optimization_barrier((picture_embeddings, text_rows))
    column, ends = join(
        (text_rows, move(text_rows, dx=1), move(text_rows, dx=-1), move(text_rows, dx=2)),
        (move(text_a, dz=2), move(text_b, dz=-2)),
    )
    unit_image, inv_image = normalize_rows(pictures)
    image_rows = unit_image.astype(jnp.bfloat16)
    other_rows = move(image_rows, swap=1)
    below, above = move(column, dz=1), move(column, dz=-1)
    far = [ends, move(ends, dx=1), move(ends, dx=-1), move(ends, dx=2)]

    grad_other, grad_own, coef, copies, total = pair_terms(
        scalars, place, other_rows, image_rows, column, below, above, far
    )

    quarter = count // 4
    received = move(grad_other, swap=1)
    parts = [
        (grad_own[k * quarter : (k + 1) * quarter] + received[k * quarter : (k + 1) * quarter]).astype(SEND)
        for k in range(4)
    ]
    total = total[:4]
    for bit in (0, 3, 4):
        total += lax.ppermute(total, AXES, [(i, i ^ (1 << bit)) for i in range(256)])
    own_sums = sums_rows(total, width)
    arrived = [move(jnp.concatenate([part, own_sums]), dy=dy) for part, dy in zip(parts[1:], (1, -1, 2))]

    coef, copies, parts[0] = lax.optimization_barrier((coef, copies, parts[0]))
    blocks = [
        lax.dot_general(coef[k], copies, (((0,), (0,)), ((), ())), preferred_element_type=jnp.float32).astype(SEND)
        for k in range(4)
    ]
    x_terms = [blocks[0], move(blocks[1], dx=-1), move(blocks[2], dx=1), move(blocks[3], dx=2)]

    y_sum = sum(part[:quarter].astype(jnp.float32) for part in [parts[0]] + arrived).astype(SEND)
    total = ring_sum(sums_of(own_sums), *[sums_of(message) for message in arrived])
    y_sum = lax.optimization_barrier(jnp.concatenate([y_sum, sums_rows(total, width)]))
    z_sum = move(y_sum, dz=4)
    total = sums_of(y_sum) + sums_of(z_sum)
    image_grad = y_sum[:quarter].astype(jnp.float32) + z_sum[:quarter].astype(jnp.float32)
    unit_part = lax.dynamic_slice_in_dim(unit_image, y * quarter, quarter)
    tangent = (image_grad - unit_part * jnp.sum(unit_part * image_grad, axis=1, keepdims=True)).astype(SEND)
    tangent = lax.optimization_barrier(tangent)
    tangents = [tangent] + [move(tangent, dy=dy) for dy in (1, -1, 2)]

    n = caption_embeddings.shape[0]
    h = n // 2
    *x_terms, tangents[1] = lax.optimization_barrier((*x_terms, tangents[1]))
    x_sum = sum(term.astype(jnp.float32) for term in x_terms).astype(SEND)
    own_sums = sums_rows(total, width)
    ride = lambda rows: jnp.concatenate([rows, own_sums])
    near = [move(ride(x_sum[n : 2 * n]), dz=-1), move(ride(x_sum[2 * n : 3 * n]), dz=1)]
    ends_sum = [move(ride(x_sum[3 * n : 3 * n + h]), dz=-2), move(x_sum[3 * n + h :], dz=2)]

    slope = jnp.zeros((count, width), SEND)
    for dy, got in zip((0, 1, -1, 2), tangents):
        slope = lax.dynamic_update_slice_in_dim(slope, got, ((y - dy) % 4) * quarter, 0)
    picture_embedding_slope = slope.astype(jnp.float32) * (temperature * inv_image)
    picture_embedding_slope, near[0], near[1], ends_sum[0], ends_sum[1] = lax.optimization_barrier(
        (picture_embedding_slope, *near, *ends_sum)
    )

    total = ring_sum(*[sums_of(message) for message in (own_sums, near[0], near[1], ends_sum[0])])
    text_sum = x_sum[:n].astype(jnp.float32) + jnp.concatenate([ends_sum[0][:h], ends_sum[1]]).astype(jnp.float32)
    text_sum += near[0][:n].astype(jnp.float32) + near[1][:n].astype(jnp.float32)
    unit_text, inv_text = normalize_rows(caption_embeddings)
    text_grad = (text_sum - unit_text * jnp.sum(unit_text * text_sum, axis=1, keepdims=True)) * (
        temperature * inv_text
    )

    rows_overall = count * lax.axis_size("blk")
    scale = jnp.where(jnp.arange(3) == 1, temperature, 1.0) / (STAT_SCALE * rows_overall)
    statistics = total[:3, 0] * scale
    return (picture_embedding_slope, text_grad, statistics)


def solution(mesh):
    placed = (P("blk", None), P(("group", "blk"), None), P(), P())
    return jax.shard_map(
        per_device,
        mesh=mesh,
        in_specs=placed,
        out_specs=(P("blk", None), P(("group", "blk"), None), P()),
        check_vma=False,
    )
```

```python
import jax
import jax.numpy as jnp
from jax import lax
from jax.experimental import pallas as pl
from jax.experimental.pallas import tpu as pltpu
from jax.sharding import PartitionSpec as P

AXES = ("group", "blk")
SEND = jnp.float16
STAT_SCALE = 2.0**-14
VMEM_BYTES = 28 * 1024 * 1024
PAIR_VMEM_BYTES = 28 * 1024 * 1024
SMEM = pl.BlockSpec(memory_space=pltpu.SMEM)
HBM = pl.BlockSpec(memory_space=pltpu.HBM)


def device_index(z, y, x, core):
    return (((z // 4) * 4 + y) * 4 + x) * 8 + (z % 4) * 2 + core


def shifted(dz=0, dy=0, dx=0, swap=0):
    pairs = []
    for z in range(8):
        for y in range(4):
            for x in range(4):
                for core in range(2):
                    there = device_index((z + dz) % 8, (y + dy) % 4, (x + dx) % 4, core ^ swap)
                    pairs.append((device_index(z, y, x, core), there))
    return pairs


def move(value, **shift):
    return lax.ppermute(value, AXES, shifted(**shift))


def sums_rows(total, width):
    high = lax.optimization_barrier(total.astype(SEND))
    low = (total - high.astype(jnp.float32)).astype(SEND)
    sums = jnp.pad(jnp.concatenate([high, low]), ((0, 0), (0, width - total.shape[1])))
    return lax.optimization_barrier(sums)


def ring_sum(own, ahead, behind, far):
    return (own + far) + (ahead + behind)


def sums_of(message):
    high, low = message[-8:-4, :128], message[-4:, :128]
    return high.astype(jnp.float32) + low.astype(jnp.float32)


def normalize_rows(matrix):
    inverse_norm = lax.rsqrt(jnp.sum(matrix * matrix, axis=1, keepdims=True) + 1e-06)
    return (matrix * inverse_norm, inverse_norm)


def text_kernel(text_ref, rows_ref, a_ref, b_ref):
    text = text_ref[...]
    rows = (text * lax.rsqrt(jnp.sum(text * text, axis=1, keepdims=True) + 1e-06)).astype(jnp.bfloat16)
    half = a_ref.shape[0]
    rows_ref[...] = rows
    a_ref[...] = rows[:half]
    b_ref[...] = rows[half:]


def text_messages(texts):
    n, width = texts.shape
    shape = lambda rows: jax.ShapeDtypeStruct((rows, width), jnp.bfloat16)
    return pl.pallas_call(
        text_kernel,
        grid=(1,),
        in_specs=[pl.BlockSpec((n, width), lambda i: (0, 0))],
        out_specs=[pl.BlockSpec((rows, width), lambda i: (0, 0)) for rows in (n, n // 2, n // 2)],
        out_shape=[shape(n), shape(n // 2), shape(n // 2)],
        compiler_params=pltpu.CompilerParams(vmem_limit_bytes=VMEM_BYTES),
        name="text_rows",
    )(texts)


def run_copies(pairs, sems):
    copies = [pltpu.make_async_copy(source, target, sems.at[i]) for i, (source, target) in enumerate(pairs)]
    for copy in copies:
        copy.start()
    for copy in copies:
        copy.wait()


def join_kernel(*refs):
    parts, (column_ref, ends_ref, sems) = refs[:-3], refs[-3:]
    pairs = []
    for out_ref, sources in ((column_ref, parts[:4]), (ends_ref, parts[4:])):
        start = 0
        for ref in sources:
            pairs.append((ref, out_ref.at[start : start + ref.shape[0], :]))
            start += ref.shape[0]
    run_copies(pairs, sems)


def join(column, ends):
    width = column[0].shape[1]
    heights = [sum(part.shape[0] for part in parts) for parts in (column, ends)]
    return pl.pallas_call(
        join_kernel,
        grid=(1,),
        in_specs=[HBM] * 6,
        out_specs=[pl.BlockSpec((rows, width), lambda i: (0, 0)) for rows in heights],
        out_shape=[jax.ShapeDtypeStruct((rows, width), column[0].dtype) for rows in heights],
        scratch_shapes=[pltpu.SemaphoreType.DMA((6,))],
        compiler_params=pltpu.CompilerParams(vmem_limit_bytes=PAIR_VMEM_BYTES),
        name="join",
    )(*column, *ends)


def text_index(place_ref, texts):
    lane = lax.broadcasted_iota(jnp.int32, (1, texts), 1)
    column, part, row = lane >> 8, (lane >> 6) & 3, lane & 63
    dx = jnp.where(column == 1, -1, column - (column >> 1))
    far = jnp.where(row < 32, -2, 2)
    dz = jnp.where(part == 3, far, jnp.where(part == 2, 1, -part))
    z = (place_ref[0] + dz) & 7
    x = (place_ref[2] + dx) & 3
    device = (z >> 2) * 128 + place_ref[1] * 32 + x * 8 + (z & 3) * 2 + place_ref[3]
    return device * 64 + row


def pair_block(scal_ref, image, text, row_ids, text_ids, stat_ref):
    products = lax.dot_general(image, text, (((1,), (1,)), ((), ())), preferred_element_type=jnp.float32)
    logits = scal_ref[0] * products + scal_ref[1]
    paired = row_ids == text_ids
    grown = jnp.exp(logits)
    above = 1.0 + grown
    coeff = jnp.where(paired, -1.0, grown) * pl.reciprocal(above)
    loss = jnp.where(grown < 1e-3, grown * (1.0 - 0.5 * grown), jnp.log(above))
    loss = loss - jnp.where(paired, logits, 0.0)
    width = products.shape[1]
    stat_ref[0] += jnp.sum(loss.reshape(-1, 8, width), axis=0)
    stat_ref[1] += jnp.sum((coeff * products).reshape(-1, 8, width), axis=0)
    stat_ref[2] += jnp.sum(coeff.reshape(-1, 8, width), axis=0)
    return coeff.astype(jnp.bfloat16)


def pair_kernel(side, scal_ref, place_ref, image_ref, *rest):
    if side == 0:
        pieces, rest = rest[:7], rest[7:]
        grad_ref, coef_ref, copy_ref, text_ref, stat_ref, sems = rest
    else:
        text_ref, sums_ref, _, _, grad_ref, coef_ref, copy_ref, total_ref, stat_ref, sems = rest
    count = image_ref.shape[0]
    quarter = count // 4
    columns = coef_ref.shape[2]
    block = columns // 4
    starts = [pl.multiple_of(((place_ref[1] + dy) & 3) * quarter, quarter) for dy in (0, 1, 3, 2)]
    pairs = [
        (image_ref.at[pl.ds(start, quarter), :], copy_ref.at[i * quarter : (i + 1) * quarter, :])
        for i, start in enumerate(starts)
    ]
    if side == 0:
        for k in range(4):
            for j in range(4):
                piece = pieces[j].at[block * k : block * (k + 1), :] if j < 3 else pieces[3 + k]
                at = columns * k + block * j
                pairs.append((piece, text_ref.at[at : at + block, :]))
    run_copies(pairs, sems)
    stat_ref[...] = jnp.zeros_like(stat_ref) if side == 0 else sums_ref[...]
    text = text_ref[...]
    ids = text_index(place_ref, text.shape[0])
    row_iota = lax.broadcasted_iota(jnp.int32, (quarter, 1), 0) + place_ref[4 + side]
    for half in range(2):
        rows = slice(2 * half * quarter, 2 * (half + 1) * quarter)
        row_ids = jnp.concatenate([row_iota + start for start in starts[2 * half : 2 * half + 2]])
        coeff = pair_block(scal_ref, copy_ref[rows, :], text, row_ids, ids, stat_ref)
        grad_ref[rows, :] = jnp.dot(coeff, text, preferred_element_type=jnp.float32)
        for k in range(4):
            coef_ref[k, rows, :] = coeff[:, k * columns : (k + 1) * columns]
    if side == 1:
        total_ref[...] = jnp.zeros_like(total_ref)
        for k in range(3):
            stat = stat_ref[k]
            lanes = sum(stat[:, 128 * i : 128 * (i + 1)] for i in range(stat.shape[1] // 128))
            each = jnp.sum(jnp.sum(lanes, axis=0, keepdims=True), axis=1, keepdims=True)
            total_ref[k : k + 1, :] = jnp.broadcast_to(each * STAT_SCALE, (1, 128))


def pair_terms(scalars, place, other, own, col, below, above, far):
    count, width = own.shape
    texts = 4 * col.shape[0]
    f32, bf16 = jnp.float32, jnp.bfloat16
    shape = jax.ShapeDtypeStruct
    cost = pl.CostEstimate(
        flops=4 * count * texts * width, bytes_accessed=12 * count * width, transcendentals=3 * count * texts
    )
    params = pltpu.CompilerParams(vmem_limit_bytes=PAIR_VMEM_BYTES)
    whole = lambda *dims: pl.BlockSpec(dims, lambda i: (0,) * len(dims))
    coef_shape, copy_shape = shape((4, 2 * count, texts // 4), bf16), shape((2 * count, width), bf16)
    stat = (3, 8, texts)
    grad_other, coef, copies, text, sums = pl.pallas_call(
        lambda *refs: pair_kernel(0, *refs),
        grid=(1,),
        in_specs=[SMEM, SMEM] + [HBM] * 8,
        out_specs=[
            whole(count, width),
            whole(4, count, texts // 4),
            whole(count, width),
            whole(texts, width),
            whole(*stat),
        ],
        out_shape=[shape((count, width), f32), coef_shape, copy_shape, shape((texts, width), bf16), shape(stat, f32)],
        scratch_shapes=[pltpu.SemaphoreType.DMA((20,))],
        compiler_params=params,
        cost_estimate=cost,
        name="other_rows",
    )(scalars, place, other, col, below, above, *far)
    grad_own, coef, copies, total = pl.pallas_call(
        lambda *refs: pair_kernel(1, *refs),
        grid=(1,),
        in_specs=[SMEM, SMEM, HBM, whole(texts, width), whole(*stat), HBM, HBM],
        out_specs=[
            whole(count, width),
            pl.BlockSpec((4, count, texts // 4), lambda i: (0, 1, 0)),
            pl.BlockSpec((count, width), lambda i: (1, 0)),
            whole(8, 128),
        ],
        out_shape=[shape((count, width), f32), coef_shape, copy_shape, shape((8, 128), f32)],
        scratch_shapes=[pltpu.VMEM(stat, f32), pltpu.SemaphoreType.DMA((4,))],
        input_output_aliases={5: 1, 6: 2},
        compiler_params=params,
        cost_estimate=cost,
        name="own_rows",
    )(scalars, place, own, text, sums, coef, copies)
    return grad_other, grad_own, coef, copies, total


def per_device(picture_embeddings, caption_embeddings, exponent_of_sharpness, offset_shift):
    count, width = picture_embeddings.shape
    group, blk = lax.axis_index("group"), lax.axis_index("blk")
    z, y, x, core = (group // 4) * 4 + (blk // 2) % 4, group % 4, blk // 8, blk % 2
    temperature = jnp.exp(exponent_of_sharpness[0])
    scalars = jnp.stack([temperature, offset_shift[0]])
    place = jnp.stack([z, y, x, core, (blk ^ 1) * count, blk * count]).astype(jnp.int32)

    text_rows, text_a, text_b = text_messages(caption_embeddings)
    pictures, text_rows = lax.optimization_barrier((picture_embeddings, text_rows))
    column, ends = join(
        (text_rows, move(text_rows, dx=1), move(text_rows, dx=-1), move(text_rows, dx=2)),
        (move(text_a, dz=2), move(text_b, dz=-2)),
    )
    unit_image, inv_image = normalize_rows(pictures)
    image_rows = unit_image.astype(jnp.bfloat16)
    other_rows = move(image_rows, swap=1)
    below, above = move(column, dz=1), move(column, dz=-1)
    far = [ends, move(ends, dx=1), move(ends, dx=-1), move(ends, dx=2)]

    grad_other, grad_own, coef, copies, total = pair_terms(
        scalars, place, other_rows, image_rows, column, below, above, far
    )

    quarter = count // 4
    received = move(grad_other, swap=1)
    total = total[:4]
    total += move(total, swap=1)
    total = ring_sum(total, move(total, dx=1), move(total, dx=-1), move(total, dx=2))
    grad_own, received, total = lax.optimization_barrier((grad_own, received, total))
    parts = [
        (grad_own[k * quarter : (k + 1) * quarter] + received[k * quarter : (k + 1) * quarter]).astype(SEND)
        for k in range(4)
    ]
    own_sums = sums_rows(total, width)
    arrived = [move(jnp.concatenate([part, own_sums]), dy=dy) for part, dy in zip(parts[1:], (1, -1, 2))]

    coef, copies, parts[0] = lax.optimization_barrier((coef, copies, parts[0]))
    blocks = [
        lax.dot_general(coef[k], copies, (((0,), (0,)), ((), ())), preferred_element_type=jnp.float32).astype(SEND)
        for k in range(4)
    ]
    x_terms = [blocks[0], move(blocks[1], dx=-1), move(blocks[2], dx=1), move(blocks[3], dx=2)]

    y_sum = sum(part[:quarter].astype(jnp.float32) for part in [parts[0]] + arrived).astype(SEND)
    total = ring_sum(sums_of(own_sums), *[sums_of(message) for message in arrived])
    y_sum = lax.optimization_barrier(jnp.concatenate([y_sum, sums_rows(total, width)]))
    z_sum = move(y_sum, dz=4)
    total = sums_of(y_sum) + sums_of(z_sum)
    image_grad = y_sum[:quarter].astype(jnp.float32) + z_sum[:quarter].astype(jnp.float32)
    unit_part = lax.dynamic_slice_in_dim(unit_image, y * quarter, quarter)
    tangent = (image_grad - unit_part * jnp.sum(unit_part * image_grad, axis=1, keepdims=True)).astype(SEND)
    tangent = lax.optimization_barrier(tangent)
    tangents = [tangent] + [move(tangent, dy=dy) for dy in (1, -1, 2)]

    n = caption_embeddings.shape[0]
    h = n // 2
    *x_terms, tangents[1] = lax.optimization_barrier((*x_terms, tangents[1]))
    x_sum = sum(term.astype(jnp.float32) for term in x_terms).astype(SEND)
    own_sums = sums_rows(total, width)
    ride = lambda rows: jnp.concatenate([rows, own_sums])
    near = [move(ride(x_sum[n : 2 * n]), dz=-1), move(ride(x_sum[2 * n : 3 * n]), dz=1)]
    ends_sum = [move(ride(x_sum[3 * n : 3 * n + h]), dz=-2), move(x_sum[3 * n + h :], dz=2)]

    slope = jnp.zeros((count, width), SEND)
    for dy, got in zip((0, 1, -1, 2), tangents):
        slope = lax.dynamic_update_slice_in_dim(slope, got, ((y - dy) % 4) * quarter, 0)
    picture_embedding_slope = slope.astype(jnp.float32) * (temperature * inv_image)
    picture_embedding_slope, near[0], near[1], ends_sum[0], ends_sum[1] = lax.optimization_barrier(
        (picture_embedding_slope, *near, *ends_sum)
    )

    total = ring_sum(*[sums_of(message) for message in (own_sums, near[0], near[1], ends_sum[0])])
    text_sum = x_sum[:n].astype(jnp.float32) + jnp.concatenate([ends_sum[0][:h], ends_sum[1]]).astype(jnp.float32)
    text_sum += near[0][:n].astype(jnp.float32) + near[1][:n].astype(jnp.float32)
    unit_text, inv_text = normalize_rows(caption_embeddings)
    text_grad = (text_sum - unit_text * jnp.sum(unit_text * text_sum, axis=1, keepdims=True)) * (
        temperature * inv_text
    )

    rows_overall = count * lax.axis_size("blk")
    scale = jnp.where(jnp.arange(3) == 1, temperature, 1.0) / (STAT_SCALE * rows_overall)
    statistics = total[:3, 0] * scale
    return (picture_embedding_slope, text_grad, statistics)


def solution(mesh):
    placed = (P("blk", None), P(("group", "blk"), None), P(), P())
    return jax.shard_map(
        per_device,
        mesh=mesh,
        in_specs=placed,
        out_specs=(P("blk", None), P(("group", "blk"), None), P()),
        check_vma=False,
    )
```
